32 devices in a mesh: group: 2 (over y), gx: 4 (over z), gy: 2 (over x), sec: 2 (over core).
Axes of the slice: x: 2, y: 2, z: 4, core: 2. Of those that a mesh axis runs over, the one named last changes fastest.
Arguments:
- pressure: float32 [2, 32, 32, 128], P('sec', ('group', 'gx'), 'gy'), parts along dimension 1, may hold values from -6 to 6
- pressure_before: float32 [2, 32, 32, 128], P('sec', ('group', 'gx'), 'gy'), parts along dimension 1, may hold values from -6 to 6
- quasi: float32 [2, 32, 32, 128], P('sec', ('group', 'gx'), 'gy'), parts along dimension 1, may hold values from -6 to 6
- quasi_before: float32 [2, 32, 32, 128], P('sec', ('group', 'gx'), 'gy'), parts along dimension 1, may hold values from -6 to 6
- courant: float32 [16, 32, 128], P('gx', 'gy'), may hold values from 0.02 to 0.08
- epsilon: float32 [16, 32, 128], P('gx', 'gy'), may hold values from 0 to 0.3
- delta: float32 [16, 32, 128], P('gx', 'gy'), may hold values from -0.1 to 0.2
- tilt: float32 [16, 32, 128], P('gx', 'gy'), may hold values from -3.140625 to 3.140625
- azimuth: float32 [16, 32, 128], P('gx', 'gy'), may hold values from -3.140625 to 3.140625
- plan: int32 [4], replicated, may hold values from 1 to 8, as said below
- lags: int32 [5], replicated, may hold values from -4 to 4, as said below
Outputs:
- pressure_final: float32 [2, 32, 32, 128], P('sec', ('group', 'gx'), 'gy'), parts along dimension 1
- quasi_final: float32 [2, 32, 32, 128], P('sec', ('group', 'gx'), 'gy'), parts along dimension 1
- image: float32 [5, 32, 32, 128], P(None, ('group', 'gx'), 'gy', 'sec'), parts along dimension 1
The draws below stay inside these ranges and needn't reach their ends.
There are 2 independent parts, one for each index of `group`. The reference program is written for one: setup_inputs(seed, part) draws one part's arguments, and reference() takes and returns one part's arrays. A program takes and returns all parts, laid end to end along the dimension named above; an argument that names none is the same for every part. Nothing has to cross between parts.
Inputs may be any that keep to these rules, and one draw needn't show every extreme that they name: `plan`: distinct steps in rising order; the last entry is 8. Distinct lags; the first is -4 and the last 4.
All inputs are finite; a program needn't handle non-finite values.
Results may differ from the reference program's by a relative error of at most 0.0001.
Values sent between devices are 32-bit elements; how exact they have to be, the bound alone decides.
No kernel may reach another device: no remote copies, remote signals or barrier semaphores. Data moves between devices by JAX's collectives and lax.ppermute only.
A program may use at most 64 MiB of HBM per device.

```python
import math
import jax
import jax.numpy as jnp
from jax import lax

NZ = 128
STEPS = 8
NSNAP = 4
HOFF = 5
LAGMAX = 4
NX = 16
NY = 32


def draw_plan(key, part):
    candidates = jnp.arange(1, STEPS, dtype=jnp.int32)
    earlier = jax.random.permutation(jax.random.fold_in(key, 11), candidates)[:NSNAP - 1]
    earlier = jnp.sort(earlier.astype(jnp.int32))
    return jnp.concatenate([earlier, jnp.full((1,), STEPS, jnp.int32)])


def draw_lags(key, part):
    middle_values = jnp.arange(-(LAGMAX - 1), LAGMAX, dtype=jnp.int32)
    chosen = jax.random.permutation(jax.random.fold_in(key, 23), middle_values)[:HOFF - 2]
    return jnp.concatenate([jnp.full((1,), -LAGMAX, jnp.int32), chosen.astype(jnp.int32), jnp.full((1,), LAGMAX, jnp.int32)])


def block_levels(key, dims, shards, low, high):
    factor_of, own = 1.0, jax.random.fold_in(key, 6)
    for position, blocks in shards:
        heights = jnp.exp(jax.random.uniform(jax.random.fold_in(own, position), (blocks,), jnp.float32, low / len(shards), high / len(shards)))
        factor_of = factor_of * jnp.repeat(heights, dims[position] // blocks).reshape([-1 if axis == position else 1 for axis in range(len(dims))])
    return factor_of


def scatter_about(rng, extent, deviation, limit, pieces=(), held_as=jnp.bfloat16):
    level = block_levels(rng, extent, pieces, -0.22, 0.18) if pieces else 1.0
    values = jax.random.normal(rng, extent, jnp.float32) * deviation * level
    return jnp.minimum(jnp.maximum(values, -limit), limit).astype(held_as)


def setup_inputs(seed: int = 0, part: int = 0) -> dict:
    key_of = jax.random.split(jax.random.key(seed), 12)
    part_keys = jax.random.split(jax.random.fold_in(key_of[11], part), 12)
    return {
        "pressure": scatter_about(part_keys[0], (2, NX, NY, NZ), 1.0, 6.0, ((0, 2), (1, 4), (2, 2)), jnp.float32),
        "pressure_before": scatter_about(part_keys[1], (2, NX, NY, NZ), 1.0, 6.0, ((0, 2), (1, 4), (2, 2)), jnp.float32),
        "quasi": scatter_about(part_keys[2], (2, NX, NY, NZ), 1.0, 6.0, ((0, 2), (1, 4), (2, 2)), jnp.float32),
        "quasi_before": scatter_about(part_keys[3], (2, NX, NY, NZ), 1.0, 6.0, ((0, 2), (1, 4), (2, 2)), jnp.float32),
        "courant": jnp.clip(jnp.exp(math.log(0.08) - 1.3862944 * jax.random.uniform(key_of[4], (NX, NY, NZ), jnp.float32) ** block_levels(key_of[4], (NX, NY, NZ), ((0, 4), (1, 2)), -0.2, 0.2)), 0.02, 0.08),
        "epsilon": jnp.clip(0.3 * jax.random.uniform(key_of[5], (NX, NY, NZ), jnp.float32) ** block_levels(key_of[5], (NX, NY, NZ), ((0, 4), (1, 2)), -0.2, 0.2), 0.0, 0.3),
        "delta": jnp.clip(-0.1 + 0.3 * jax.random.uniform(key_of[6], (NX, NY, NZ), jnp.float32) ** block_levels(key_of[6], (NX, NY, NZ), ((0, 4), (1, 2)), -0.2, 0.2), -0.1, 0.2),
        "tilt": jnp.clip(jax.random.uniform(key_of[7], (NX, NY, NZ), jnp.float32, -3.140625, 3.140625), -3.140625, 3.140625),
        "azimuth": jnp.clip(jax.random.uniform(key_of[8], (NX, NY, NZ), jnp.float32, -3.140625, 3.140625), -3.140625, 3.140625),
        "plan": draw_plan(jax.random.fold_in(key_of[11], 71), part),
        "lags": draw_lags(jax.random.fold_in(key_of[11], 71), part),
    }


SECOND = (-205.0 / 72.0, 8.0 / 5.0, -1.0 / 5.0, 8.0 / 315.0, -1.0 / 560.0)
FIRST = (4.0 / 5.0, -1.0 / 5.0, 4.0 / 105.0, -1.0 / 280.0)


def second_along(values, dimension):
    amount = values.shape[dimension] - 8
    result = SECOND[0] * lax.slice_in_dim(values, 4, 4 + amount, axis=dimension)
    for offset in range(1, 5):
        result = result + SECOND[offset] * (lax.slice_in_dim(values, 4 + offset, 4 + offset + amount, axis=dimension) + lax.slice_in_dim(values, 4 - offset, 4 - offset + amount, axis=dimension))
    return result


def first_along(values, dimension):
    amount = values.shape[dimension] - 8
    result = FIRST[0] * (lax.slice_in_dim(values, 5, 5 + amount, axis=dimension) - lax.slice_in_dim(values, 3, 3 + amount, axis=dimension))
    for offset in range(2, 5):
        result = result + FIRST[offset - 1] * (lax.slice_in_dim(values, 4 + offset, 4 + offset + amount, axis=dimension) - lax.slice_in_dim(values, 4 - offset, 4 - offset + amount, axis=dimension))
    return result


def trimmed(values, dimensions):
    for dimension in dimensions:
        values = lax.slice_in_dim(values, 4, values.shape[dimension] - 4, axis=dimension)
    return values


def orientation(tilt, azimuth):
    sin_tilt = jnp.sin(tilt)
    cos_tilt = jnp.cos(tilt)
    sin_azim = jnp.sin(azimuth)
    cos_azim = jnp.cos(azimuth)
    square_sin = sin_tilt * sin_tilt
    double_tilt = jnp.sin(2.0 * tilt)
    return (square_sin * cos_azim * cos_azim, square_sin * sin_azim * sin_azim, cos_tilt * cos_tilt,
            square_sin * jnp.sin(2.0 * azimuth), double_tilt * sin_azim, double_tilt * cos_azim)


def tilted_terms(padded, weights):
    curve_xx = trimmed(second_along(padded, 1), (2, 3))
    curve_yy = trimmed(second_along(padded, 2), (1, 3))
    curve_zz = trimmed(second_along(padded, 3), (1, 2))
    slope_x = first_along(padded, 1)
    slope_y = first_along(padded, 2)
    curve_xy = trimmed(first_along(slope_x, 2), (3,))
    curve_xz = trimmed(first_along(slope_x, 3), (2,))
    curve_yz = trimmed(first_along(slope_y, 3), (1,))
    axial = (weights[0] * curve_xx + weights[1] * curve_yy + weights[2] * curve_zz
             + weights[3] * curve_xy + weights[4] * curve_yz + weights[5] * curve_xz)
    laplace = curve_xx + curve_yy + curve_zz
    return axial, laplace


def advance(now_p, before_p, now_q, before_q, axial_p, laplace_p, axial_q, courant, epsilon, delta):
    flat_p = laplace_p - axial_p
    next_p = 2.0 * now_p - before_p + courant * ((1.0 + 2.0 * epsilon) * flat_p + axial_q)
    next_q = 2.0 * now_q - before_q + courant * ((1.0 + 2.0 * delta) * flat_p + axial_q)
    return next_p, next_q


def reference(pressure, pressure_before, quasi, quasi_before, courant, epsilon, delta, tilt, azimuth, plan, lags):
    weights = orientation(tilt, azimuth)
    snapshots = jnp.zeros((2, NSNAP, NX, NY, NZ), jnp.float32)
    for step in range(STEPS):
        stacked = jnp.concatenate([pressure, quasi], 0)
        padded = jnp.pad(stacked, ((0, 0), (4, 4), (4, 4), (4, 4)))
        axial, laplace = tilted_terms(padded, weights)
        next_p, next_q = advance(pressure, pressure_before, quasi, quasi_before,
                                 axial[0:2], laplace[0:2], axial[2:4], courant, epsilon, delta)
        pressure_before, quasi_before = pressure, quasi
        pressure, quasi = next_p, next_q
        picked = (plan == step + 1).astype(jnp.float32)
        snapshots = snapshots + picked[None, :, None, None, None] * pressure[:, None]
    padded_snaps = jnp.pad(snapshots, ((0, 0), (0, 0), (LAGMAX, LAGMAX), (0, 0), (0, 0)))
    images = []
    for offset_index in range(HOFF):
        lag_cells = lags[offset_index].astype(jnp.int32)
        source = lax.dynamic_slice_in_dim(padded_snaps[0], (LAGMAX - lag_cells).astype(jnp.int32), NX, 1)
        receiver = lax.dynamic_slice_in_dim(padded_snaps[1], (LAGMAX + lag_cells).astype(jnp.int32), NX, 1)
        images.append(jnp.sum(source * receiver, axis=0))
    return pressure, quasi, jnp.stack(images)
```

```python
import functools

import jax
import jax.numpy as jnp
import numpy as np
from jax import lax
from jax.experimental import pallas as pl
from jax.experimental.pallas import tpu as pltpu
from jax.sharding import PartitionSpec as P

STEPS = 8
REACH = 4
ROWS = 8

SECOND = (-205.0 / 72.0, 8.0 / 5.0, -1.0 / 5.0, 8.0 / 315.0, -1.0 / 560.0)
FIRST = (4.0 / 5.0, -1.0 / 5.0, 4.0 / 105.0, -1.0 / 280.0)
SECOND_TAIL = tuple(c / SECOND[1] for c in SECOND[2:])
FIRST_TAIL = tuple(b / FIRST[0] for b in FIRST[1:])
SECOND_SCALE = 5040.0 / 8192.0
FIRST_SCALE = 840.0 / 1024.0


def depth_matrix(depth):
    second = np.zeros((depth, depth))
    first = np.zeros((depth, depth))
    for m in range(1, REACH + 1):
        second += SECOND_SCALE * SECOND[m] * (np.eye(depth, k=m) + np.eye(depth, k=-m))
        first += FIRST_SCALE * FIRST[m - 1] * (np.eye(depth, k=-m) - np.eye(depth, k=m))
    both = np.concatenate([second, first], axis=1)
    return jnp.asarray(np.concatenate([both, both], axis=0), jnp.bfloat16)


def swapped(block, axis, bit):
    count = lax.axis_size(axis)
    return lax.ppermute(block, axis, [(i, i ^ bit) for i in range(count)])


def window(place, tile, halo, total, unit):
    count = total // tile
    length = 0
    for i in range(count):
        low = max(0, i * tile - halo) // unit * unit
        high = -(-min(total, (i + 1) * tile + halo) // unit) * unit
        length = max(length, high - low)
    start = jnp.clip((place * tile - halo) // unit * unit, 0, total - length)
    return start, length


def pair_sums(load, tail):
    total = load(1) + load(-1)
    for m, c in enumerate(tail, 2):
        total = total + c * (load(m) + load(-m))
    return total


def pair_differences(load, tail):
    total = load(1) - load(-1)
    for m, b in enumerate(tail, 2):
        total = total + b * (load(m) - load(-m))
    return total


def steps_kernel(sizes, plan_ref, place_ref, matrix_ref, *refs):
    tile_x, tile_y, total_x, total_y, depth, slots, nsnap = sizes
    tiles = refs[: len(slots)]
    halves = refs[len(slots)]
    p_out, q_out, snap_out = refs[len(slots) + 1 : len(slots) + 4]
    pa, pb, qa, qb, first_z, second_z, slope_x, weights = refs[len(slots) + 4 :]
    gx, gy, sec = place_ref[0], place_ref[1], place_ref[2]
    half = tile_x // 2

    full_y = total_y + 2 * ROWS
    for ref in (pa, pb, qa, qb, first_z.at[0], first_z.at[1]):
        for start in (0, total_x + REACH):
            ref[start : start + REACH] = jnp.zeros((REACH, full_y, depth), jnp.float32)
        for start in (0, total_y + ROWS):
            ref[:, start : start + ROWS] = jnp.zeros((total_x + 2 * REACH, ROWS, depth), jnp.float32)
    for start in (0, total_y + ROWS):
        slope_x[:, start : start + ROWS] = jnp.zeros((2, ROWS, depth), jnp.float32)

    for slot, (kx, ky) in enumerate(slots):
        ix, iy = jnp.bitwise_xor(gx, kx), jnp.bitwise_xor(gy, ky)
        xs = ix * tile_x
        ys = pl.multiple_of(iy * tile_y, ROWS)
        for number, ref in enumerate((pa, pb, qa, qb)):
            ref[pl.ds(xs + REACH, tile_x), pl.ds(pl.multiple_of(ys + ROWS, ROWS), tile_y)] = tiles[slot][
                number * tile_x : (number + 1) * tile_x
            ]
        for side in (0, 1):
            source = halves.at[slot] if side else tiles[slot].at[4 * tile_x :]
            base = xs + half * (jnp.bitwise_xor(sec, side))
            for row in range(half):
                courant, epsilon, delta, tilt, azimuth = (source[g * half + row] for g in range(5))
                sin_t, cos_t = jnp.sin(tilt), jnp.cos(tilt)
                sin_a, cos_a = jnp.sin(azimuth), jnp.cos(azimuth)
                axis_x, axis_y = sin_t * cos_a, sin_t * sin_a
                cross = courant * (2.0 * FIRST[0] / FIRST_SCALE)
                fields = (
                    courant * SECOND[1] * axis_x * axis_x,
                    courant * SECOND[1] * axis_y * axis_y,
                    courant * (1.0 / SECOND_SCALE) * cos_t * cos_t,
                    courant * (2.0 * FIRST[0] * FIRST[0]) * axis_x * axis_y,
                    cross * axis_y * cos_t,
                    cross * axis_x * cos_t,
                    courant * SECOND[1],
                    1.0 + 2.0 * epsilon,
                    1.0 + 2.0 * delta,
                )
                for number, field in enumerate(fields):
                    weights[number, base + row, pl.ds(ys, tile_y)] = field

    matrix = matrix_ref[...]
    now, before = (pa, qa), (pb, qb)
    for step in range(1, STEPS + 1):
        left = REACH * (STEPS - step)
        x_low = jnp.maximum(gx * tile_x - left - REACH, 0)
        x_high = jnp.minimum((gx + 1) * tile_x + left + REACH, total_x)
        y_low, y_length = window(gy, tile_y, left, total_y, ROWS)
        if y_length == total_y:
            y_low = 0
        slope_length = min(y_length + 2 * ROWS, total_y)
        slope_low = 0 if slope_length == total_y else jnp.clip(y_low - ROWS, 0, total_y - slope_length)
        z_low = jnp.maximum(x_low - REACH, 0) // REACH
        z_high = jnp.minimum(x_high + REACH, total_x) // REACH

        def depth_body(block, carry, now=now):
            x = block * REACH
            rows = REACH * total_y
            parts = [
                ref[pl.ds(x + REACH, REACH), ROWS : ROWS + total_y].reshape(rows, depth) for ref in now
            ]
            both = jnp.concatenate(parts, axis=0)
            high = both.astype(jnp.bfloat16)
            low = (both - high.astype(jnp.float32)).astype(jnp.bfloat16)
            out = jnp.dot(
                jnp.concatenate([high, low], axis=1), matrix, preferred_element_type=jnp.float32
            )
            for f in (0, 1):
                piece = out[f * rows : (f + 1) * rows]
                second_z[f, pl.ds(x, REACH)] = piece[:, :depth].reshape(REACH, total_y, depth)
                first_z[f, pl.ds(x + REACH, REACH), ROWS : ROWS + total_y] = piece[:, depth:].reshape(
                    REACH, total_y, depth
                )
            return carry

        lax.fori_loop(z_low, z_high, depth_body, 0)

        def row_body(x, carry, now=now, before=before, y_low=y_low, y_length=y_length,
                     slope_low=slope_low, slope_length=slope_length):
            row = x + REACH
            for f in (0, 1):
                for j in range(0, slope_length, ROWS):
                    ys = pl.ds(ROWS + slope_low + j, ROWS)
                    load = lambda m: now[f][row + m, ys]
                    slope_x[f, ys] = pair_differences(load, FIRST_TAIL)
            for j in range(0, y_length, ROWS):
                at = y_low + j
                ys = pl.ds(at, ROWS)
                here = ROWS + at
                w = [weights[i, x, ys] for i in range(9)]
                axial = []
                for f in (0, 1):
                    along_x = lambda m: now[f][row + m, pl.ds(here, ROWS)]
                    along_y = lambda m: now[f][row, pl.ds(here + m, ROWS)]
                    curve_xx = pair_sums(along_x, SECOND_TAIL)
                    curve_yy = pair_sums(along_y, SECOND_TAIL)
                    curve_zz = second_z[f, x, ys]
                    curve_xy = pair_differences(lambda m: slope_x[f, pl.ds(here + m, ROWS)], FIRST_TAIL)
                    curve_yz = pair_differences(
                        lambda m: first_z[f, row, pl.ds(here + m, ROWS)], FIRST_TAIL
                    )
                    curve_xz = pair_differences(
                        lambda m: first_z[f, row + m, pl.ds(here, ROWS)], FIRST_TAIL
                    )
                    axial.append(
                        w[0] * curve_xx + w[1] * curve_yy + w[2] * curve_zz
                        + w[3] * curve_xy + w[4] * curve_yz + w[5] * curve_xz
                    )
                    if f == 0:
                        laplace = curve_xx + curve_yy + curve_zz * (1.0 / (SECOND_SCALE * SECOND[1]))
                p = now[0][row, pl.ds(here, ROWS)]
                q = now[1][row, pl.ds(here, ROWS)]
                flat = w[6] * (laplace + (2.0 * SECOND[0] / SECOND[1]) * p) - axial[0]
                shared = axial[1] + w[6] * ((SECOND[0] / SECOND[1]) * q)
                spot = (row, pl.ds(here, ROWS))
                before[0][spot] = 2.0 * p - before[0][spot] + w[7] * flat + shared
                before[1][spot] = 2.0 * q - before[1][spot] + w[8] * flat + shared
            return carry

        lax.fori_loop(x_low, x_high, row_body, 0)
        now, before = before, now

        mine = pl.ds(pl.multiple_of(ROWS + gy * tile_y, ROWS), tile_y)
        for j in range(nsnap):
            @pl.when(plan_ref[j] == step)
            def _():
                snap_out[j] = now[0][pl.ds(gx * tile_x, tile_x + 2 * REACH), mine]

    p_out[0] = now[0][pl.ds(gx * tile_x + REACH, tile_x), mine]
    q_out[0] = now[1][pl.ds(gx * tile_x + REACH, tile_x), mine]


def image_kernel(lags_ref, place_ref, own_ref, other_ref, image_ref):
    sec = place_ref[2]
    sign = 1 - 2 * sec
    nlag, tile_x, tile_y, half = image_ref.shape
    nsnap = own_ref.shape[0]
    for k in range(nlag):
        shift = sign * lags_ref[k]
        total = own_ref[0, pl.ds(REACH - shift, tile_x)] * other_ref[0, pl.ds(REACH + shift, tile_x)]
        for j in range(1, nsnap):
            total = total + own_ref[j, pl.ds(REACH - shift, tile_x)] * other_ref[j, pl.ds(REACH + shift, tile_x)]
        flat = total.reshape(tile_x * tile_y, 2 * half)
        chosen = jnp.where(sec == 0, flat, pltpu.roll(flat, half, 1))
        image_ref[k] = chosen[:, :half].reshape(tile_x, tile_y, half)


def gathered_solution(pressure, pressure_before, quasi, quasi_before, courant, epsilon, delta, tilt, azimuth, plan, lags):
    count_x, count_y = lax.axis_size("gx"), lax.axis_size("gy")
    gx, gy, sec = lax.axis_index("gx"), lax.axis_index("gy"), lax.axis_index("sec")
    _, tile_x, tile_y, depth = pressure.shape
    total_x, total_y = count_x * tile_x, count_y * tile_y
    half = tile_x // 2
    place = jnp.stack([gx, gy, sec]).astype(jnp.int32)

    waves = jnp.concatenate([pressure[0], pressure_before[0], quasi[0], quasi_before[0]])
    earth = jnp.stack([courant, epsilon, delta, tilt, azimuth])
    earth = lax.dynamic_slice_in_dim(earth, sec * half, half, 1).reshape(5 * half, tile_y, depth)
    held = {(0, 0): jnp.concatenate([waves, earth])}
    for ky in range(count_y):
        if ky:
            low = ky & -ky
            held[0, ky] = swapped(held[0, ky ^ low], "gy", low)
    for kx in range(1, count_x):
        low = kx & -kx
        rest = kx ^ low
        held[kx, 0] = swapped(held[rest, 0] if rest else held[0, 0], "gx", low)
    for kx in range(1, count_x):
        for ky in range(1, count_y):
            low = ky & -ky
            held[kx, ky] = swapped(held[kx, ky ^ low], "gy", low)
    slots = tuple(held)
    tiles = list(held.values())
    other = swapped(jnp.stack([t[4 * tile_x :] for t in tiles]), "sec", 1)

    nsnap = plan.shape[0]
    sizes = (tile_x, tile_y, total_x, total_y, depth, slots, nsnap)
    vmem = pl.BlockSpec(memory_space=pltpu.VMEM)
    smem = pl.BlockSpec(memory_space=pltpu.SMEM)
    field = pltpu.VMEM((total_x + 2 * REACH, total_y + 2 * ROWS, depth), jnp.float32)
    p_final, q_final, snaps = pl.pallas_call(
        functools.partial(steps_kernel, sizes),
        out_shape=(
            jax.ShapeDtypeStruct(pressure.shape, jnp.float32),
            jax.ShapeDtypeStruct(quasi.shape, jnp.float32),
            jax.ShapeDtypeStruct((nsnap, tile_x + 2 * REACH, tile_y, depth), jnp.float32),
        ),
        in_specs=[smem, smem, vmem] + [vmem] * (len(tiles) + 1),
        out_specs=(vmem, vmem, vmem),
        scratch_shapes=[
            field, field, field, field,
            pltpu.VMEM((2, total_x + 2 * REACH, total_y + 2 * ROWS, depth), jnp.float32),
            pltpu.VMEM((2, total_x, total_y, depth), jnp.float32),
            pltpu.VMEM((2, total_y + 2 * ROWS, depth), jnp.float32),
            pltpu.VMEM((9, total_x, total_y, depth), jnp.float32),
        ],
        compiler_params=pltpu.CompilerParams(vmem_limit_bytes=40 * 1024 * 1024),
    )(plan, place, depth_matrix(depth), *tiles, other)

    other_snaps = swapped(snaps, "sec", 1)
    image = pl.pallas_call(
        image_kernel,
        out_shape=jax.ShapeDtypeStruct((lags.shape[0], tile_x, tile_y, depth // 2), jnp.float32),
        in_specs=[smem, smem, vmem, vmem],
        out_specs=vmem,
    )(lags, place, snaps, other_snaps)
    return (p_final, q_final, image)


def with_halo(cells, sides, width):
    for axis, dim in sides:
        count = lax.axis_size(axis)
        ends = count - 1
        head = lax.slice_in_dim(cells, 0, width, axis=dim)
        tail = lax.slice_in_dim(cells, cells.shape[dim] - width, cells.shape[dim], axis=dim)
        cells = jnp.concatenate(
            [
                lax.ppermute(tail, axis, [(i, (i + 1) % count) for i in range(ends)]),
                cells,
                lax.ppermute(head, axis, [((i + 1) % count, i) for i in range(ends)]),
            ],
            axis=dim,
        )
    return cells


def from_behind(block, axis, distance):
    devices = range(lax.axis_size(axis))
    route = [(i - distance, i) for i in devices if i - distance in devices]
    return lax.ppermute(block, axis, route)


def second_along(values, dimension):
    amount = values.shape[dimension] - 8
    result = SECOND[0] * lax.slice_in_dim(values, 4, 4 + amount, axis=dimension)
    for offset in range(1, 5):
        result = result + SECOND[offset] * (
            lax.slice_in_dim(values, 4 + offset, 4 + offset + amount, axis=dimension)
            + lax.slice_in_dim(values, 4 - offset, 4 - offset + amount, axis=dimension)
        )
    return result


def first_along(values, dimension):
    amount = values.shape[dimension] - 8
    result = FIRST[0] * (
        lax.slice_in_dim(values, 5, 5 + amount, axis=dimension)
        - lax.slice_in_dim(values, 3, 3 + amount, axis=dimension)
    )
    for offset in range(2, 5):
        result = result + FIRST[offset - 1] * (
            lax.slice_in_dim(values, 4 + offset, 4 + offset + amount, axis=dimension)
            - lax.slice_in_dim(values, 4 - offset, 4 - offset + amount, axis=dimension)
        )
    return result


def trimmed(values, dimensions):
    for dimension in dimensions:
        values = lax.slice_in_dim(values, 4, values.shape[dimension] - 4, axis=dimension)
    return values


def orientation(tilt, azimuth):
    sin_tilt = jnp.sin(tilt)
    cos_tilt = jnp.cos(tilt)
    sin_azim = jnp.sin(azimuth)
    cos_azim = jnp.cos(azimuth)
    square_sin = sin_tilt * sin_tilt
    double_tilt = jnp.sin(2.0 * tilt)
    return (
        square_sin * cos_azim * cos_azim,
        square_sin * sin_azim * sin_azim,
        cos_tilt * cos_tilt,
        square_sin * jnp.sin(2.0 * azimuth),
        double_tilt * sin_azim,
        double_tilt * cos_azim,
    )


def tilted_terms(padded, weights):
    curve_xx = trimmed(second_along(padded, 1), (2, 3))
    curve_yy = trimmed(second_along(padded, 2), (1, 3))
    curve_zz = trimmed(second_along(padded, 3), (1, 2))
    slope_x = first_along(padded, 1)
    slope_y = first_along(padded, 2)
    curve_xy = trimmed(first_along(slope_x, 2), (3,))
    curve_xz = trimmed(first_along(slope_x, 3), (2,))
    curve_yz = trimmed(first_along(slope_y, 3), (1,))
    axial = (
        weights[0] * curve_xx
        + weights[1] * curve_yy
        + weights[2] * curve_zz
        + weights[3] * curve_xy
        + weights[4] * curve_yz
        + weights[5] * curve_xz
    )
    laplace = curve_xx + curve_yy + curve_zz
    return (axial, laplace)


def advance(now_p, before_p, now_q, before_q, axial_p, laplace_p, axial_q, courant, epsilon, delta):
    flat_p = laplace_p - axial_p
    next_p = 2.0 * now_p - before_p + courant * ((1.0 + 2.0 * epsilon) * flat_p + axial_q)
    next_q = 2.0 * now_q - before_q + courant * ((1.0 + 2.0 * delta) * flat_p + axial_q)
    return (next_p, next_q)


def offset_image(paired, lags):
    rim_width = paired.shape[2]
    padded = with_halo(paired, (("gx", 2),), rim_width)
    images = []
    for offset_index in range(lags.shape[0]):
        lag_cells = lags[offset_index]
        source = lax.dynamic_slice_in_dim(padded[0], rim_width - lag_cells, rim_width, 1)
        receiver = lax.dynamic_slice_in_dim(padded[1], rim_width + lag_cells, rim_width, 1)
        images.append(jnp.sum(source * receiver, axis=0))
    return jnp.stack(images)


def stepwise_solution(pressure, pressure_before, quasi, quasi_before, courant, epsilon, delta, tilt, azimuth, plan, lags):
    weights = orientation(tilt, azimuth)
    snapshots = jnp.zeros((plan.shape[0],) + pressure.shape[1:], jnp.float32)
    for step in range(STEPS):
        stacked = jnp.concatenate([pressure, quasi], 0)
        padded = with_halo(stacked, (("gx", 1), ("gy", 2)), 4)
        padded = jnp.pad(padded, ((0, 0), (0, 0), (0, 0), (4, 4)))
        axial, laplace = tilted_terms(padded, weights)
        next_p, next_q = advance(
            pressure, pressure_before, quasi, quasi_before,
            axial[0:1], laplace[0:1], axial[1:2], courant, epsilon, delta,
        )
        pressure_before, quasi_before = (pressure, quasi)
        pressure, quasi = (next_p, next_q)
        picked = (plan == step + 1).astype(jnp.float32)
        snapshots = snapshots + picked[:, None, None, None] * pressure
    arrived = from_behind(snapshots, "sec", 1)
    paired = jnp.stack([arrived, snapshots])
    whole_image = offset_image(paired, lags)
    half_depth = whole_image.shape[3] // 2
    returned = from_behind(whole_image[..., :half_depth], "sec", -1)
    image = jnp.where(lax.axis_index("sec") == 0, returned, whole_image[..., half_depth:])
    return (pressure, quasi, image)


def on_device(*args):
    count_x, count_y = lax.axis_size("gx"), lax.axis_size("gy")
    _, tile_x, tile_y, depth = args[0].shape
    cells = count_x * tile_x * count_y * tile_y * depth
    fits = (
        cells <= 1 << 17
        and count_x & (count_x - 1) == 0
        and count_y & (count_y - 1) == 0
        and tile_x % REACH == 0
        and tile_y % ROWS == 0
        and depth == 128
    )
    return (gathered_solution if fits else stepwise_solution)(*args)


def solution(mesh):
    wave = P("sec", ("group", "gx"), "gy", None)
    earth = P("gx", "gy", None)
    return jax.shard_map(
        on_device,
        mesh=mesh,
        in_specs=(wave,) * 4 + (earth,) * 5 + (P(), P()),
        out_specs=(wave, wave, P(None, ("group", "gx"), "gy", "sec")),
        check_vma=False,
    )
```

```python
import functools
import math

import jax
import jax.numpy as jnp
import numpy as np
from jax import lax
from jax.experimental import pallas as pl
from jax.experimental.pallas import tpu as pltpu
from jax.sharding import PartitionSpec as P

STEPS = 8
REACH = 4
ROWS = 8
UNROLL = 4

SECOND = (-205.0 / 72.0, 8.0 / 5.0, -1.0 / 5.0, 8.0 / 315.0, -1.0 / 560.0)
FIRST = (4.0 / 5.0, -1.0 / 5.0, 4.0 / 105.0, -1.0 / 280.0)
SECOND_TAIL = tuple(c / SECOND[1] for c in SECOND[2:])
FIRST_TAIL = tuple(b / FIRST[0] for b in FIRST[1:])
SECOND_SCALE = 5040.0 / 8192.0
FIRST_SCALE = 840.0 / 1024.0


def depth_matrix(depth):
    second = np.zeros((depth, depth))
    first = np.zeros((depth, depth))
    for m in range(1, REACH + 1):
        second += SECOND_SCALE * SECOND[m] * (np.eye(depth, k=m) + np.eye(depth, k=-m))
        first += FIRST_SCALE * FIRST[m - 1] * (np.eye(depth, k=-m) - np.eye(depth, k=m))
    both = np.concatenate([second, first], axis=1)
    return jnp.asarray(np.concatenate([both, both], axis=0), jnp.bfloat16)


def sine_cosine(angle):
    half = 0.5 * angle
    square = half * half

    def series(first, count):
        value = jnp.full_like(square, (-1) ** (count - 1) / math.factorial(2 * count - 2 + first))
        for k in range(count - 2, -1, -1):
            value = value * square + (-1) ** k / math.factorial(2 * k + first)
        return value

    sine = half * series(1, 7)
    return 2.0 * sine * series(0, 8), 1.0 - 2.0 * sine * sine


def swapped(block, axis, bit):
    count = lax.axis_size(axis)
    return lax.ppermute(block, axis, [(i, i ^ bit) for i in range(count)])


def window(place, tile, halo, total, unit):
    count = total // tile
    length = 0
    for i in range(count):
        low = max(0, i * tile - halo) // unit * unit
        high = -(-min(total, (i + 1) * tile + halo) // unit) * unit
        length = max(length, high - low)
    start = jnp.clip((place * tile - halo) // unit * unit, 0, total - length)
    return start, length


def pair_sums(load, tail):
    total = load(1) + load(-1)
    for m, c in enumerate(tail, 2):
        total = total + c * (load(m) + load(-m))
    return total


def pair_differences(load, tail):
    total = load(1) - load(-1)
    for m, b in enumerate(tail, 2):
        total = total + b * (load(m) - load(-m))
    return total


def pack_kernel(*refs):
    waves, earth, out_ref, sems = refs[:4], refs[4:9], refs[9], refs[10]
    tile_x = waves[0].shape[1]
    half = tile_x // 2
    first = lax.axis_index("sec") * half
    copies = []
    for number, ref in enumerate(waves):
        copies.append((ref.at[0], out_ref.at[pl.ds(number * tile_x, tile_x)]))
    for number, ref in enumerate(earth):
        copies.append((ref.at[pl.ds(first, half)], out_ref.at[pl.ds(4 * tile_x + number * half, half)]))
    copies = [pltpu.make_async_copy(a, b, sems.at[i]) for i, (a, b) in enumerate(copies)]
    for copy in copies:
        copy.start()
    for copy in copies:
        copy.wait()


def steps_kernel(sizes, plan_ref, matrix_ref, *refs):
    tile_x, tile_y, total_x, total_y, depth, slots, nsnap = sizes
    tiles = refs[: len(slots)]
    halves = refs[len(slots)]
    p_out, q_out, snap_out = refs[len(slots) + 1 : len(slots) + 4]
    pa, pb, qa, qb, first_a, first_b, second_a, second_b, slope_x, weights = refs[len(slots) + 4 :]
    gx, gy, sec = lax.axis_index("gx"), lax.axis_index("gy"), lax.axis_index("sec")
    half = tile_x // 2

    full_y = total_y + 2 * ROWS
    for ref in (pa, pb, qa, qb, first_a.at[0], first_a.at[1], first_b.at[0], first_b.at[1]):
        for start in (0, total_x + REACH):
            ref[start : start + REACH] = jnp.zeros((REACH, full_y, depth), jnp.float32)
        for start in (0, total_y + ROWS):
            ref[:, start : start + ROWS] = jnp.zeros((total_x + 2 * REACH, ROWS, depth), jnp.float32)
    for start in (0, total_y + ROWS):
        slope_x[:, start : start + ROWS] = jnp.zeros((2 * UNROLL, ROWS, depth), jnp.float32)

    for slot, (kx, ky) in enumerate(slots):
        ix, iy = jnp.bitwise_xor(gx, kx), jnp.bitwise_xor(gy, ky)
        xs = ix * tile_x
        ys = pl.multiple_of(iy * tile_y, ROWS)
        for number, ref in enumerate((pa, pb, qa, qb)):
            ref[pl.ds(xs + REACH, tile_x), pl.ds(pl.multiple_of(ys + ROWS, ROWS), tile_y)] = tiles[slot][
                number * tile_x : (number + 1) * tile_x
            ]
        for side in (0, 1):
            source = halves.at[slot] if side else tiles[slot].at[4 * tile_x :]
            base = xs + half * (jnp.bitwise_xor(sec, side))
            for row in range(half):
                courant, epsilon, delta, tilt, azimuth = (source[g * half + row] for g in range(5))
                sin_t, cos_t = sine_cosine(tilt)
                sin_a, cos_a = sine_cosine(azimuth)
                axis_x, axis_y = sin_t * cos_a, sin_t * sin_a
                cross = courant * (2.0 * FIRST[0] / FIRST_SCALE)
                fields = (
                    courant * SECOND[1] * axis_x * axis_x,
                    courant * SECOND[1] * axis_y * axis_y,
                    courant * (1.0 / SECOND_SCALE) * cos_t * cos_t,
                    courant * (2.0 * FIRST[0] * FIRST[0]) * axis_x * axis_y,
                    cross * axis_y * cos_t,
                    cross * axis_x * cos_t,
                    courant * SECOND[1],
                    1.0 + 2.0 * epsilon,
                    1.0 + 2.0 * delta,
                )
                for number, field in enumerate(fields):
                    weights[number, base + row, pl.ds(ys, tile_y)] = field

    matrix = matrix_ref[...]

    def depth_rows(x, count, fields, first_z, second_z):
        size = count * total_y
        parts = [ref[pl.ds(x + REACH, count), ROWS : ROWS + total_y].reshape(size, depth) for ref in fields]
        both = jnp.concatenate(parts, axis=0)
        high = both.astype(jnp.bfloat16)
        low = (both - high.astype(jnp.float32)).astype(jnp.bfloat16)
        out = jnp.dot(jnp.concatenate([high, low], axis=1), matrix, preferred_element_type=jnp.float32)
        for f in (0, 1):
            piece = out[f * size : (f + 1) * size]
            second_z[f, pl.ds(x + REACH, count)] = piece[:, :depth].reshape(count, total_y, depth)
            first_z[f, pl.ds(x + REACH, count), ROWS : ROWS + total_y] = piece[:, depth:].reshape(
                count, total_y, depth
            )

    now, before = (pa, qa), (pb, qb)
    along_z, along_z_next = (first_a, second_a), (first_b, second_b)

    def start_body(block, carry):
        depth_rows(block * REACH, REACH, (pa, qa), first_a, second_a)
        return carry

    lax.fori_loop(0, total_x // REACH, start_body, 0)

    for step in range(1, STEPS + 1):
        left = REACH * (STEPS - step)
        x_low = jnp.maximum(gx * tile_x - left - REACH, 0)
        x_high = jnp.minimum((gx + 1) * tile_x + left + REACH, total_x)
        y_low, y_length = window(gy, tile_y, left, total_y, ROWS)
        if y_length == total_y:
            y_low = 0
        slope_length = min(y_length + 2 * ROWS, total_y)
        slope_low = 0 if slope_length == total_y else jnp.clip(y_low - ROWS, 0, total_y - slope_length)
        first_z, second_z = along_z

        def one_row(x, lane, now, before, y_low, y_length, slope_low, slope_length, first_z, second_z):
            row = x + REACH
            kept = {}
            for f in (0, 1):
                for j in range(0, slope_length, ROWS):
                    ys = pl.ds(ROWS + slope_low + j, ROWS)
                    near = {m: now[f][row + m, ys] for m in range(-REACH, REACH + 1) if m}
                    slope_x[2 * lane + f, ys] = pair_differences(near.get, FIRST_TAIL)
                    if y_length == total_y:
                        kept[f, j] = pair_sums(near.get, SECOND_TAIL)
            for j in range(0, y_length, ROWS):
                at = y_low + j
                ys = pl.ds(at, ROWS)
                here = ROWS + at
                w = [weights[i, x, ys] for i in range(9)]
                axial = []
                for f in (0, 1):
                    if (f, j) in kept:
                        curve_xx = kept[f, j]
                    else:
                        curve_xx = pair_sums(lambda m: now[f][row + m, pl.ds(here, ROWS)], SECOND_TAIL)
                    curve_yy = pair_sums(lambda m: now[f][row, pl.ds(here + m, ROWS)], SECOND_TAIL)
                    curve_zz = second_z[f, row, ys]
                    curve_xy = pair_differences(
                        lambda m: slope_x[2 * lane + f, pl.ds(here + m, ROWS)], FIRST_TAIL
                    )
                    curve_yz = pair_differences(
                        lambda m: first_z[f, row, pl.ds(here + m, ROWS)], FIRST_TAIL
                    )
                    curve_xz = pair_differences(
                        lambda m: first_z[f, row + m, pl.ds(here, ROWS)], FIRST_TAIL
                    )
                    axial.append(
                        w[0] * curve_xx + w[1] * curve_yy + w[2] * curve_zz
                        + w[3] * curve_xy + w[4] * curve_yz + w[5] * curve_xz
                    )
                    if f == 0:
                        laplace = curve_xx + curve_yy + curve_zz * (1.0 / (SECOND_SCALE * SECOND[1]))
                p = now[0][row, pl.ds(here, ROWS)]
                q = now[1][row, pl.ds(here, ROWS)]
                flat = w[6] * (laplace + (2.0 * SECOND[0] / SECOND[1]) * p) - axial[0]
                shared = axial[1] + w[6] * ((SECOND[0] / SECOND[1]) * q)
                spot = (row, pl.ds(here, ROWS))
                before[0][spot] = 2.0 * p - before[0][spot] + w[7] * flat + shared
                before[1][spot] = 2.0 * q - before[1][spot] + w[8] * flat + shared

        def rows_body(block, carry, step=step, now=now, before=before, y_low=y_low, y_length=y_length,
                      slope_low=slope_low, slope_length=slope_length, along_z=along_z, ahead=along_z_next):
            x = block * UNROLL
            if step < STEPS:
                depth_rows(x - UNROLL, UNROLL, before, *ahead)
            for lane in range(UNROLL):
                one_row(x + lane, lane, now, before, y_low, y_length, slope_low, slope_length, *along_z)
            return carry

        lax.fori_loop(x_low // UNROLL, x_high // UNROLL, rows_body, 0)
        if step < STEPS:
            depth_rows(x_high - UNROLL, UNROLL, before, *along_z_next)
        now, before = before, now
        along_z, along_z_next = along_z_next, along_z

        mine = pl.ds(pl.multiple_of(ROWS + gy * tile_y, ROWS), tile_y)
        for j in range(nsnap):
            @pl.when(plan_ref[j] == step)
            def _():
                snap_out[j] = now[0][pl.ds(gx * tile_x, tile_x + 2 * REACH), mine]

    p_out[0] = now[0][pl.ds(gx * tile_x + REACH, tile_x), mine]
    q_out[0] = now[1][pl.ds(gx * tile_x + REACH, tile_x), mine]


def image_kernel(lags_ref, own_ref, other_ref, image_ref):
    sec = lax.axis_index("sec")
    sign = 1 - 2 * sec
    nlag, tile_x, tile_y, half = image_ref.shape
    nsnap = own_ref.shape[0]
    for k in range(nlag):
        shift = sign * lags_ref[k]
        total = own_ref[0, pl.ds(REACH - shift, tile_x)] * other_ref[0, pl.ds(REACH + shift, tile_x)]
        for j in range(1, nsnap):
            total = total + own_ref[j, pl.ds(REACH - shift, tile_x)] * other_ref[j, pl.ds(REACH + shift, tile_x)]
        flat = total.reshape(tile_x * tile_y, 2 * half)
        chosen = jnp.where(sec == 0, flat, pltpu.roll(flat, half, 1))
        image_ref[k] = chosen[:, :half].reshape(tile_x, tile_y, half)


def gathered_solution(pressure, pressure_before, quasi, quasi_before, courant, epsilon, delta, tilt, azimuth, plan, lags):
    count_x, count_y = lax.axis_size("gx"), lax.axis_size("gy")
    _, tile_x, tile_y, depth = pressure.shape
    total_x, total_y = count_x * tile_x, count_y * tile_y
    half = tile_x // 2
    vmem = pl.BlockSpec(memory_space=pltpu.VMEM)
    smem = pl.BlockSpec(memory_space=pltpu.SMEM)
    apart = pl.BlockSpec(memory_space=pl.ANY)

    parts = (pressure, pressure_before, quasi, quasi_before, courant, epsilon, delta, tilt, azimuth)
    packed = pl.pallas_call(
        pack_kernel,
        out_shape=jax.ShapeDtypeStruct((4 * tile_x + 5 * half, tile_y, depth), jnp.float32),
        in_specs=[apart] * len(parts),
        out_specs=vmem,
        scratch_shapes=[pltpu.SemaphoreType.DMA((len(parts),))],
    )(*parts)
    held = {(0, 0): packed}
    for ky in range(count_y):
        if ky:
            low = ky & -ky
            held[0, ky] = swapped(held[0, ky ^ low], "gy", low)
    for kx in range(1, count_x):
        low = kx & -kx
        rest = kx ^ low
        held[kx, 0] = swapped(held[rest, 0] if rest else held[0, 0], "gx", low)
    for kx in range(1, count_x):
        for ky in range(1, count_y):
            low = ky & -ky
            held[kx, ky] = swapped(held[kx, ky ^ low], "gy", low)
    slots = tuple(held)
    tiles = list(held.values())
    other = swapped(jnp.stack([t[4 * tile_x :] for t in tiles]), "sec", 1)

    nsnap = plan.shape[0]
    sizes = (tile_x, tile_y, total_x, total_y, depth, slots, nsnap)
    field = pltpu.VMEM((total_x + 2 * REACH, total_y + 2 * ROWS, depth), jnp.float32)
    slope = pltpu.VMEM((2, total_x + 2 * REACH, total_y + 2 * ROWS, depth), jnp.float32)
    curve = pltpu.VMEM((2, total_x + 2 * REACH, total_y, depth), jnp.float32)
    p_final, q_final, snaps = pl.pallas_call(
        functools.partial(steps_kernel, sizes),
        out_shape=(
            jax.ShapeDtypeStruct(pressure.shape, jnp.float32),
            jax.ShapeDtypeStruct(quasi.shape, jnp.float32),
            jax.ShapeDtypeStruct((nsnap, tile_x + 2 * REACH, tile_y, depth), jnp.float32),
        ),
        in_specs=[smem, vmem] + [vmem] * (len(tiles) + 1),
        out_specs=(vmem, vmem, vmem),
        scratch_shapes=[
            field, field, field, field,
            slope, slope, curve, curve,
            pltpu.VMEM((2 * UNROLL, total_y + 2 * ROWS, depth), jnp.float32),
            pltpu.VMEM((9, total_x, total_y, depth), jnp.float32),
        ],
        compiler_params=pltpu.CompilerParams(vmem_limit_bytes=40 * 1024 * 1024),
    )(plan, depth_matrix(depth), *tiles, other)

    other_snaps = swapped(snaps, "sec", 1)
    image = pl.pallas_call(
        image_kernel,
        out_shape=jax.ShapeDtypeStruct((lags.shape[0], tile_x, tile_y, depth // 2), jnp.float32),
        in_specs=[smem, vmem, vmem],
        out_specs=vmem,
    )(lags, snaps, other_snaps)
    return (p_final, q_final, image)


def with_halo(cells, sides, width):
    for axis, dim in sides:
        count = lax.axis_size(axis)
        ends = count - 1
        head = lax.slice_in_dim(cells, 0, width, axis=dim)
        tail = lax.slice_in_dim(cells, cells.shape[dim] - width, cells.shape[dim], axis=dim)
        cells = jnp.concatenate(
            [
                lax.ppermute(tail, axis, [(i, (i + 1) % count) for i in range(ends)]),
                cells,
                lax.ppermute(head, axis, [((i + 1) % count, i) for i in range(ends)]),
            ],
            axis=dim,
        )
    return cells


def from_behind(block, axis, distance):
    devices = range(lax.axis_size(axis))
    route = [(i - distance, i) for i in devices if i - distance in devices]
    return lax.ppermute(block, axis, route)


def second_along(values, dimension):
    amount = values.shape[dimension] - 8
    result = SECOND[0] * lax.slice_in_dim(values, 4, 4 + amount, axis=dimension)
    for offset in range(1, 5):
        result = result + SECOND[offset] * (
            lax.slice_in_dim(values, 4 + offset, 4 + offset + amount, axis=dimension)
            + lax.slice_in_dim(values, 4 - offset, 4 - offset + amount, axis=dimension)
        )
    return result


def first_along(values, dimension):
    amount = values.shape[dimension] - 8
    result = FIRST[0] * (
        lax.slice_in_dim(values, 5, 5 + amount, axis=dimension)
        - lax.slice_in_dim(values, 3, 3 + amount, axis=dimension)
    )
    for offset in range(2, 5):
        result = result + FIRST[offset - 1] * (
            lax.slice_in_dim(values, 4 + offset, 4 + offset + amount, axis=dimension)
            - lax.slice_in_dim(values, 4 - offset, 4 - offset + amount, axis=dimension)
        )
    return result


def trimmed(values, dimensions):
    for dimension in dimensions:
        values = lax.slice_in_dim(values, 4, values.shape[dimension] - 4, axis=dimension)
    return values


def orientation(tilt, azimuth):
    sin_tilt = jnp.sin(tilt)
    cos_tilt = jnp.cos(tilt)
    sin_azim = jnp.sin(azimuth)
    cos_azim = jnp.cos(azimuth)
    square_sin = sin_tilt * sin_tilt
    double_tilt = jnp.sin(2.0 * tilt)
    return (
        square_sin * cos_azim * cos_azim,
        square_sin * sin_azim * sin_azim,
        cos_tilt * cos_tilt,
        square_sin * jnp.sin(2.0 * azimuth),
        double_tilt * sin_azim,
        double_tilt * cos_azim,
    )


def tilted_terms(padded, weights):
    curve_xx = trimmed(second_along(padded, 1), (2, 3))
    curve_yy = trimmed(second_along(padded, 2), (1, 3))
    curve_zz = trimmed(second_along(padded, 3), (1, 2))
    slope_x = first_along(padded, 1)
    slope_y = first_along(padded, 2)
    curve_xy = trimmed(first_along(slope_x, 2), (3,))
    curve_xz = trimmed(first_along(slope_x, 3), (2,))
    curve_yz = trimmed(first_along(slope_y, 3), (1,))
    axial = (
        weights[0] * curve_xx
        + weights[1] * curve_yy
        + weights[2] * curve_zz
        + weights[3] * curve_xy
        + weights[4] * curve_yz
        + weights[5] * curve_xz
    )
    laplace = curve_xx + curve_yy + curve_zz
    return (axial, laplace)


def advance(now_p, before_p, now_q, before_q, axial_p, laplace_p, axial_q, courant, epsilon, delta):
    flat_p = laplace_p - axial_p
    next_p = 2.0 * now_p - before_p + courant * ((1.0 + 2.0 * epsilon) * flat_p + axial_q)
    next_q = 2.0 * now_q - before_q + courant * ((1.0 + 2.0 * delta) * flat_p + axial_q)
    return (next_p, next_q)


def offset_image(paired, lags):
    rim_width = paired.shape[2]
    padded = with_halo(paired, (("gx", 2),), rim_width)
    images = []
    for offset_index in range(lags.shape[0]):
        lag_cells = lags[offset_index]
        source = lax.dynamic_slice_in_dim(padded[0], rim_width - lag_cells, rim_width, 1)
        receiver = lax.dynamic_slice_in_dim(padded[1], rim_width + lag_cells, rim_width, 1)
        images.append(jnp.sum(source * receiver, axis=0))
    return jnp.stack(images)


def stepwise_solution(pressure, pressure_before, quasi, quasi_before, courant, epsilon, delta, tilt, azimuth, plan, lags):
    weights = orientation(tilt, azimuth)
    snapshots = jnp.zeros((plan.shape[0],) + pressure.shape[1:], jnp.float32)
    for step in range(STEPS):
        stacked = jnp.concatenate([pressure, quasi], 0)
        padded = with_halo(stacked, (("gx", 1), ("gy", 2)), 4)
        padded = jnp.pad(padded, ((0, 0), (0, 0), (0, 0), (4, 4)))
        axial, laplace = tilted_terms(padded, weights)
        next_p, next_q = advance(
            pressure, pressure_before, quasi, quasi_before,
            axial[0:1], laplace[0:1], axial[1:2], courant, epsilon, delta,
        )
        pressure_before, quasi_before = (pressure, quasi)
        pressure, quasi = (next_p, next_q)
        picked = (plan == step + 1).astype(jnp.float32)
        snapshots = snapshots + picked[:, None, None, None] * pressure
    arrived = from_behind(snapshots, "sec", 1)
    paired = jnp.stack([arrived, snapshots])
    whole_image = offset_image(paired, lags)
    half_depth = whole_image.shape[3] // 2
    returned = from_behind(whole_image[..., :half_depth], "sec", -1)
    image = jnp.where(lax.axis_index("sec") == 0, returned, whole_image[..., half_depth:])
    return (pressure, quasi, image)


def on_device(*args):
    count_x, count_y = lax.axis_size("gx"), lax.axis_size("gy")
    _, tile_x, tile_y, depth = args[0].shape
    cells = count_x * tile_x * count_y * tile_y * depth
    fits = (
        cells <= 1 << 17
        and count_x & (count_x - 1) == 0
        and count_y & (count_y - 1) == 0
        and tile_x % REACH == 0
        and tile_y % ROWS == 0
        and depth == 128
    )
    return (gathered_solution if fits else stepwise_solution)(*args)


def solution(mesh):
    wave = P("sec", ("group", "gx"), "gy", None)
    earth = P("gx", "gy", None)
    return jax.shard_map(
        on_device,
        mesh=mesh,
        in_specs=(wave,) * 4 + (earth,) * 5 + (P(), P()),
        out_specs=(wave, wave, P(None, ("group", "gx"), "gy", "sec")),
        check_vma=False,
    )
```

```python
import functools
import math

import jax
import jax.numpy as jnp
import numpy as np
from jax import lax
from jax.experimental import pallas as pl
from jax.experimental.pallas import tpu as pltpu
from jax.sharding import PartitionSpec as P

STEPS = 8
REACH = 4
ROWS = 8

SECOND = (-205.0 / 72.0, 8.0 / 5.0, -1.0 / 5.0, 8.0 / 315.0, -1.0 / 560.0)
FIRST = (4.0 / 5.0, -1.0 / 5.0, 4.0 / 105.0, -1.0 / 280.0)
SECOND_TAIL = tuple(c / SECOND[1] for c in SECOND[2:])
FIRST_TAIL = tuple(b / FIRST[0] for b in FIRST[1:])
SECOND_SCALE = 5040.0 / 8192.0
FIRST_SCALE = 840.0 / 1024.0


def bands(size):
    second = np.zeros((size, size))
    first = np.zeros((size, size))
    for m in range(1, REACH + 1):
        second += SECOND_SCALE * SECOND[m] * (np.eye(size, k=m) + np.eye(size, k=-m))
        first += FIRST_SCALE * FIRST[m - 1] * (np.eye(size, k=m) - np.eye(size, k=-m))
    return second, first


def depth_matrix(depth):
    second, first = bands(depth)
    both = np.concatenate([second.T, first.T], axis=1)
    return jnp.asarray(np.concatenate([both, both], axis=0), jnp.bfloat16)


def lateral_matrix(size):
    rows = [np.kron(np.eye(REACH), band) for band in bands(size)]
    return jnp.asarray(np.concatenate([np.concatenate([r, r], axis=1) for r in rows], axis=0), jnp.bfloat16)


def sine_cosine(angle):
    half = 0.5 * angle
    square = half * half

    def series(first, count):
        value = jnp.full_like(square, (-1) ** (count - 1) / math.factorial(2 * count - 2 + first))
        for k in range(count - 2, -1, -1):
            value = value * square + (-1) ** k / math.factorial(2 * k + first)
        return value

    sine = half * series(1, 7)
    return 2.0 * sine * series(0, 8), 1.0 - 2.0 * sine * sine


def swapped(block, axis, bit):
    count = lax.axis_size(axis)
    return lax.ppermute(block, axis, [(i, i ^ bit) for i in range(count)])


def window(place, tile, halo, total, unit):
    count = total // tile
    length = 0
    for i in range(count):
        low = max(0, i * tile - halo) // unit * unit
        high = -(-min(total, (i + 1) * tile + halo) // unit) * unit
        length = max(length, high - low)
    start = jnp.clip((place * tile - halo) // unit * unit, 0, total - length)
    return start, length


def pair_sums(load, tail):
    total = load(1) + load(-1)
    for m, c in enumerate(tail, 2):
        total = total + c * (load(m) + load(-m))
    return total


def pair_differences(load, tail):
    total = load(1) - load(-1)
    for m, b in enumerate(tail, 2):
        total = total + b * (load(m) - load(-m))
    return total


def pack_kernel(*refs):
    waves, earth, out_ref, sems = refs[:4], refs[4:9], refs[9], refs[10]
    tile_x = waves[0].shape[1]
    half = tile_x // 2
    first = lax.axis_index("sec") * half
    copies = []
    for number, ref in enumerate(waves):
        copies.append((ref.at[0], out_ref.at[pl.ds(number * tile_x, tile_x)]))
    for number, ref in enumerate(earth):
        copies.append((ref.at[pl.ds(first, half)], out_ref.at[pl.ds(4 * tile_x + number * half, half)]))
    copies = [pltpu.make_async_copy(a, b, sems.at[i]) for i, (a, b) in enumerate(copies)]
    for copy in copies:
        copy.start()
    for copy in copies:
        copy.wait()


def split(values):
    high = values.astype(jnp.bfloat16)
    return high, (values - high.astype(jnp.float32)).astype(jnp.bfloat16)


def steps_kernel(sizes, plan_ref, depth_ref, lateral_ref, *refs):
    tile_x, tile_y, total_x, total_y, depth, slots, nsnap = sizes
    tiles = refs[: len(slots)]
    halves = [ref.at[i] for ref in refs[len(slots) : len(slots) + 2] for i in range(ref.shape[0])]
    p_out, q_out, snap_out = refs[len(slots) + 2 : len(slots) + 5]
    pa, pb, qa, qb, slope_a, slope_b, rest_a, rest_b, weights, kept = refs[len(slots) + 5 :]
    gx, gy, sec = lax.axis_index("gx"), lax.axis_index("gy"), lax.axis_index("sec")
    half = tile_x // 2
    blocks = total_x // REACH
    size = REACH * total_y

    slopes = [ref.at[i, f] for ref in (slope_a, slope_b) for i in (0, 1) for f in (0, 1)]
    for ref in (pa, pb, qa, qb, *slopes):
        for start in (0, total_x + REACH):
            ref[start : start + REACH] = jnp.zeros((REACH, total_y, depth), jnp.float32)

    for slot, (kx, ky) in enumerate(slots):
        ix, iy = jnp.bitwise_xor(gx, kx), jnp.bitwise_xor(gy, ky)
        xs = ix * tile_x
        ys = pl.ds(pl.multiple_of(iy * tile_y, ROWS), tile_y)
        for number, ref in enumerate((pa, pb, qa, qb)):
            ref[pl.ds(xs + REACH, tile_x), ys] = tiles[slot][number * tile_x : (number + 1) * tile_x]
        for side in (0, 1):
            source = halves[slot] if side else tiles[slot].at[4 * tile_x :]
            base = xs + half * (jnp.bitwise_xor(sec, side))
            for row in range(half):
                courant, epsilon, delta, tilt, azimuth = (source[g * half + row] for g in range(5))
                sin_t, cos_t = sine_cosine(tilt)
                sin_a, cos_a = sine_cosine(azimuth)
                axis_x, axis_y = sin_t * cos_a, sin_t * sin_a
                near, curve = courant * SECOND[1], courant * (1.0 / SECOND_SCALE)
                cross = courant * (2.0 * FIRST[0] / FIRST_SCALE)
                xx, yy, zz = axis_x * axis_x, axis_y * axis_y, cos_t * cos_t
                fields = (
                    near * xx,
                    curve * yy,
                    curve * zz,
                    near - near * xx,
                    curve - curve * yy,
                    curve - curve * zz,
                    cross * axis_x * axis_y,
                    courant * (2.0 / (FIRST_SCALE * FIRST_SCALE)) * axis_y * cos_t,
                    cross * axis_x * cos_t,
                    courant * SECOND[0],
                    1.0 + 2.0 * epsilon,
                    1.0 + 2.0 * delta,
                )
                for number, field in enumerate(fields):
                    weights[number, base + row, ys] = field

    def lateral(first, last, parts):
        matrix = lateral_ref[first * size : last * size]
        return jnp.dot(matrix, jnp.concatenate(parts, axis=0), preferred_element_type=jnp.float32)

    def put(ref, number, rows, values):
        for f in (0, 1):
            ref[number, f, rows] = values[:, f * depth : (f + 1) * depth].reshape(REACH, total_y, depth)

    def prepare(block, fields, slope, rest):
        x = block * REACH
        inner, outer = pl.ds(x, REACH), pl.ds(x + REACH, REACH)
        high, low = split(jnp.concatenate([ref[outer].reshape(size, depth) for ref in fields], axis=0))
        beside = lambda v: jnp.concatenate([v[:size], v[size:]], axis=1)
        out = jnp.dot(
            jnp.concatenate([high, low], axis=1), depth_ref[...], preferred_element_type=jnp.float32
        )
        along_y = lateral(0, 2, [beside(high), beside(low)])
        along_z = beside(out[:, depth:])
        put(rest, 0, inner, along_y[:size])
        put(rest, 1, inner, beside(out[:, :depth]))
        put(slope, 0, outer, along_y[size:])
        put(slope, 1, outer, along_z)
        put(rest, 2, inner, lateral(1, 2, split(along_z)))

    def update(block, now, before, slope, rest, y_low, y_length):
        for lane in range(REACH):
            x = block * REACH + lane
            row = x + REACH
            for j in range(0, y_length, ROWS):
                ys = pl.ds(y_low + j, ROWS)
                w = [weights[i, x, ys] for i in range(12)]
                curves, shears = [], []
                for f in (0, 1):
                    curve_xx = pair_sums(lambda m: now[f][row + m, ys], SECOND_TAIL)
                    curve_xy = pair_differences(lambda m: slope[0, f, row + m, ys], FIRST_TAIL)
                    curve_xz = pair_differences(lambda m: slope[1, f, row + m, ys], FIRST_TAIL)
                    curve_yy, curve_zz, curve_yz = (rest[i, f, x, ys] for i in range(3))
                    u = w[3:6] if f == 0 else w[0:3]
                    curves.append(u[0] * curve_xx + u[1] * curve_yy + u[2] * curve_zz)
                    shears.append(w[6] * curve_xy + w[7] * curve_yz + w[8] * curve_xz)
                p, q = now[0][row, ys], now[1][row, ys]
                p = p + p
                flat = curves[0] - shears[0] + w[9] * p
                axial = curves[1] + shears[1] + w[9] * q
                before[0][row, ys] = p - before[0][row, ys] + w[10] * flat + axial
                before[1][row, ys] = (q + q) - before[1][row, ys] + w[11] * flat + axial

    mine = pl.ds(pl.multiple_of(gy * tile_y, ROWS), tile_y)

    def keep(step, field):
        slot = nsnap
        for j in range(nsnap):
            slot = jnp.where(plan_ref[j] == step, j, slot)
        kept[slot] = field[pl.ds(gx * tile_x, tile_x + 2 * REACH), mine]

    even = ((pa, qa), slope_a, rest_a)
    odd = ((pb, qb), slope_b, rest_b)
    for block in range(blocks - 1):
        prepare(block, *even)

    now, ahead, last = even, odd, blocks - 1
    for step in range(1, STEPS + 1):
        left = REACH * (STEPS - step)
        x_low, x_length = window(gx, tile_x, left + REACH, total_x, REACH)
        y_low, y_length = window(gy, tile_y, left, total_y, ROWS)
        first = 0 if x_length == total_x else x_low // REACH
        y_low = 0 if y_length == total_y else pl.multiple_of(y_low, ROWS)
        count = x_length // REACH
        if count < 3:
            prepare(last, *now)
        for number in range(count):
            update(first + number, now[0], ahead[0], now[1], now[2], y_low, y_length)
            if number == 0 and count >= 3:
                prepare(last, *now)
            if number and step < STEPS:
                prepare(first + number - 1, *ahead)
        last = first + count - 1
        now, ahead = ahead, now
        keep(step, now[0][0])

    snap_out[...] = kept[:nsnap]
    p_out[0] = now[0][0][pl.ds(gx * tile_x + REACH, tile_x), mine]
    q_out[0] = now[0][1][pl.ds(gx * tile_x + REACH, tile_x), mine]


def image_kernel(lags_ref, own_ref, other_ref, image_ref):
    sec = lax.axis_index("sec")
    sign = 1 - 2 * sec
    nlag, tile_x, tile_y, half = image_ref.shape
    nsnap = own_ref.shape[0]
    for k in range(nlag):
        shift = sign * lags_ref[k]
        total = own_ref[0, pl.ds(REACH - shift, tile_x)] * other_ref[0, pl.ds(REACH + shift, tile_x)]
        for j in range(1, nsnap):
            total = total + own_ref[j, pl.ds(REACH - shift, tile_x)] * other_ref[j, pl.ds(REACH + shift, tile_x)]
        flat = total.reshape(tile_x * tile_y, 2 * half)
        chosen = jnp.where(sec == 0, flat, pltpu.roll(flat, half, 1))
        image_ref[k] = chosen[:, :half].reshape(tile_x, tile_y, half)


def gathered_solution(pressure, pressure_before, quasi, quasi_before, courant, epsilon, delta, tilt, azimuth, plan, lags):
    count_x, count_y = lax.axis_size("gx"), lax.axis_size("gy")
    _, tile_x, tile_y, depth = pressure.shape
    total_x, total_y = count_x * tile_x, count_y * tile_y
    half = tile_x // 2
    vmem = pl.BlockSpec(memory_space=pltpu.VMEM)
    smem = pl.BlockSpec(memory_space=pltpu.SMEM)
    apart = pl.BlockSpec(memory_space=pl.ANY)

    parts = (pressure, pressure_before, quasi, quasi_before, courant, epsilon, delta, tilt, azimuth)
    packed = pl.pallas_call(
        pack_kernel,
        out_shape=jax.ShapeDtypeStruct((4 * tile_x + 5 * half, tile_y, depth), jnp.float32),
        in_specs=[apart] * len(parts),
        out_specs=vmem,
        scratch_shapes=[pltpu.SemaphoreType.DMA((len(parts),))],
    )(*parts)
    held = {(0, 0): packed}
    for ky in range(count_y):
        if ky:
            low = ky & -ky
            held[0, ky] = swapped(held[0, ky ^ low], "gy", low)
    for kx in range(1, count_x):
        low = kx & -kx
        rest = kx ^ low
        held[kx, 0] = swapped(held[rest, 0] if rest else held[0, 0], "gx", low)
    for ky in range(1, count_y):
        for kx in range(1, count_x):
            low = ky & -ky
            if kx == 1:
                held[kx, ky] = swapped(held[0, ky], "gx", 1)
            else:
                held[kx, ky] = swapped(held[kx, ky ^ low], "gy", low)
    slots = tuple(held)
    tiles = list(held.values())
    direct = [s for s in slots if 0 in s and all(k & (k - 1) == 0 for k in s)]
    relayed = [s for s in slots if s not in direct]
    slots = tuple(direct + relayed)
    tiles = [held[s] for s in slots]
    others = [swapped(jnp.stack([held[s][4 * tile_x :] for s in part]), "sec", 1) for part in (direct, relayed)]

    nsnap = plan.shape[0]
    sizes = (tile_x, tile_y, total_x, total_y, depth, slots, nsnap)
    field = pltpu.VMEM((total_x + 2 * REACH, total_y, depth), jnp.float32)
    slope = pltpu.VMEM((2, 2, total_x + 2 * REACH, total_y, depth), jnp.float32)
    rest = pltpu.VMEM((3, 2, total_x, total_y, depth), jnp.float32)
    p_final, q_final, snaps = pl.pallas_call(
        functools.partial(steps_kernel, sizes),
        out_shape=(
            jax.ShapeDtypeStruct(pressure.shape, jnp.float32),
            jax.ShapeDtypeStruct(quasi.shape, jnp.float32),
            jax.ShapeDtypeStruct((nsnap, tile_x + 2 * REACH, tile_y, depth), jnp.float32),
        ),
        in_specs=[smem, vmem, vmem] + [vmem] * (len(tiles) + 2),
        out_specs=(vmem, vmem, vmem),
        scratch_shapes=[
            field, field, field, field,
            slope, slope, rest, rest,
            pltpu.VMEM((12, total_x, total_y, depth), jnp.float32),
            pltpu.VMEM((nsnap + 1, tile_x + 2 * REACH, tile_y, depth), jnp.float32),
        ],
        compiler_params=pltpu.CompilerParams(vmem_limit_bytes=24 * 1024 * 1024),
    )(plan, depth_matrix(depth), lateral_matrix(total_y), *tiles, *others)

    other_snaps = swapped(snaps, "sec", 1)
    image = pl.pallas_call(
        image_kernel,
        out_shape=jax.ShapeDtypeStruct((lags.shape[0], tile_x, tile_y, depth // 2), jnp.float32),
        in_specs=[smem, vmem, vmem],
        out_specs=vmem,
    )(lags, snaps, other_snaps)
    return (p_final, q_final, image)


def with_halo(cells, sides, width):
    for axis, dim in sides:
        count = lax.axis_size(axis)
        ends = count - 1
        head = lax.slice_in_dim(cells, 0, width, axis=dim)
        tail = lax.slice_in_dim(cells, cells.shape[dim] - width, cells.shape[dim], axis=dim)
        cells = jnp.concatenate(
            [
                lax.ppermute(tail, axis, [(i, (i + 1) % count) for i in range(ends)]),
                cells,
                lax.ppermute(head, axis, [((i + 1) % count, i) for i in range(ends)]),
            ],
            axis=dim,
        )
    return cells


def from_behind(block, axis, distance):
    devices = range(lax.axis_size(axis))
    route = [(i - distance, i) for i in devices if i - distance in devices]
    return lax.ppermute(block, axis, route)


def second_along(values, dimension):
    amount = values.shape[dimension] - 8
    result = SECOND[0] * lax.slice_in_dim(values, 4, 4 + amount, axis=dimension)
    for offset in range(1, 5):
        result = result + SECOND[offset] * (
            lax.slice_in_dim(values, 4 + offset, 4 + offset + amount, axis=dimension)
            + lax.slice_in_dim(values, 4 - offset, 4 - offset + amount, axis=dimension)
        )
    return result


def first_along(values, dimension):
    amount = values.shape[dimension] - 8
    result = FIRST[0] * (
        lax.slice_in_dim(values, 5, 5 + amount, axis=dimension)
        - lax.slice_in_dim(values, 3, 3 + amount, axis=dimension)
    )
    for offset in range(2, 5):
        result = result + FIRST[offset - 1] * (
            lax.slice_in_dim(values, 4 + offset, 4 + offset + amount, axis=dimension)
            - lax.slice_in_dim(values, 4 - offset, 4 - offset + amount, axis=dimension)
        )
    return result


def trimmed(values, dimensions):
    for dimension in dimensions:
        values = lax.slice_in_dim(values, 4, values.shape[dimension] - 4, axis=dimension)
    return values


def orientation(tilt, azimuth):
    sin_tilt = jnp.sin(tilt)
    cos_tilt = jnp.cos(tilt)
    sin_azim = jnp.sin(azimuth)
    cos_azim = jnp.cos(azimuth)
    square_sin = sin_tilt * sin_tilt
    double_tilt = jnp.sin(2.0 * tilt)
    return (
        square_sin * cos_azim * cos_azim,
        square_sin * sin_azim * sin_azim,
        cos_tilt * cos_tilt,
        square_sin * jnp.sin(2.0 * azimuth),
        double_tilt * sin_azim,
        double_tilt * cos_azim,
    )


def tilted_terms(padded, weights):
    curve_xx = trimmed(second_along(padded, 1), (2, 3))
    curve_yy = trimmed(second_along(padded, 2), (1, 3))
    curve_zz = trimmed(second_along(padded, 3), (1, 2))
    slope_x = first_along(padded, 1)
    slope_y = first_along(padded, 2)
    curve_xy = trimmed(first_along(slope_x, 2), (3,))
    curve_xz = trimmed(first_along(slope_x, 3), (2,))
    curve_yz = trimmed(first_along(slope_y, 3), (1,))
    axial = (
        weights[0] * curve_xx
        + weights[1] * curve_yy
        + weights[2] * curve_zz
        + weights[3] * curve_xy
        + weights[4] * curve_yz
        + weights[5] * curve_xz
    )
    laplace = curve_xx + curve_yy + curve_zz
    return (axial, laplace)


def advance(now_p, before_p, now_q, before_q, axial_p, laplace_p, axial_q, courant, epsilon, delta):
    flat_p = laplace_p - axial_p
    next_p = 2.0 * now_p - before_p + courant * ((1.0 + 2.0 * epsilon) * flat_p + axial_q)
    next_q = 2.0 * now_q - before_q + courant * ((1.0 + 2.0 * delta) * flat_p + axial_q)
    return (next_p, next_q)


def offset_image(paired, lags):
    rim_width = paired.shape[2]
    padded = with_halo(paired, (("gx", 2),), rim_width)
    images = []
    for offset_index in range(lags.shape[0]):
        lag_cells = lags[offset_index]
        source = lax.dynamic_slice_in_dim(padded[0], rim_width - lag_cells, rim_width, 1)
        receiver = lax.dynamic_slice_in_dim(padded[1], rim_width + lag_cells, rim_width, 1)
        images.append(jnp.sum(source * receiver, axis=0))
    return jnp.stack(images)


def stepwise_solution(pressure, pressure_before, quasi, quasi_before, courant, epsilon, delta, tilt, azimuth, plan, lags):
    weights = orientation(tilt, azimuth)
    snapshots = jnp.zeros((plan.shape[0],) + pressure.shape[1:], jnp.float32)
    for step in range(STEPS):
        stacked = jnp.concatenate([pressure, quasi], 0)
        padded = with_halo(stacked, (("gx", 1), ("gy", 2)), 4)
        padded = jnp.pad(padded, ((0, 0), (0, 0), (0, 0), (4, 4)))
        axial, laplace = tilted_terms(padded, weights)
        next_p, next_q = advance(
            pressure, pressure_before, quasi, quasi_before,
            axial[0:1], laplace[0:1], axial[1:2], courant, epsilon, delta,
        )
        pressure_before, quasi_before = (pressure, quasi)
        pressure, quasi = (next_p, next_q)
        picked = (plan == step + 1).astype(jnp.float32)
        snapshots = snapshots + picked[:, None, None, None] * pressure
    arrived = from_behind(snapshots, "sec", 1)
    paired = jnp.stack([arrived, snapshots])
    whole_image = offset_image(paired, lags)
    half_depth = whole_image.shape[3] // 2
    returned = from_behind(whole_image[..., :half_depth], "sec", -1)
    image = jnp.where(lax.axis_index("sec") == 0, returned, whole_image[..., half_depth:])
    return (pressure, quasi, image)


def on_device(*args):
    count_x, count_y = lax.axis_size("gx"), lax.axis_size("gy")
    _, tile_x, tile_y, depth = args[0].shape
    cells = count_x * tile_x * count_y * tile_y * depth
    fits = (
        cells <= 1 << 16
        and count_x * tile_x <= 8 * REACH
        and count_x & (count_x - 1) == 0
        and count_y & (count_y - 1) == 0
        and tile_x % REACH == 0
        and tile_y % ROWS == 0
        and depth == 128
    )
    return (gathered_solution if fits else stepwise_solution)(*args)


def solution(mesh):
    wave = P("sec", ("group", "gx"), "gy", None)
    earth = P("gx", "gy", None)
    return jax.shard_map(
        on_device,
        mesh=mesh,
        in_specs=(wave,) * 4 + (earth,) * 5 + (P(), P()),
        out_specs=(wave, wave, P(None, ("group", "gx"), "gy", "sec")),
        check_vma=False,
    )
```

```python
import functools
import math

import jax
import jax.numpy as jnp
import numpy as np
from jax import lax
from jax.experimental import pallas as pl
from jax.experimental.pallas import tpu as pltpu
from jax.sharding import PartitionSpec as P

STEPS = 8
REACH = 4
ROWS = 8

SECOND = (-205.0 / 72.0, 8.0 / 5.0, -1.0 / 5.0, 8.0 / 315.0, -1.0 / 560.0)
FIRST = (4.0 / 5.0, -1.0 / 5.0, 4.0 / 105.0, -1.0 / 280.0)
SECOND_TAIL = tuple(c / SECOND[1] for c in SECOND[2:])
FIRST_TAIL = tuple(b / FIRST[0] for b in FIRST[1:])
SECOND_SCALE = 5040.0 / 8192.0
FIRST_SCALE = 840.0 / 1024.0


def bands(size):
    second = np.zeros((size, size))
    first = np.zeros((size, size))
    for m in range(1, REACH + 1):
        second += SECOND_SCALE * SECOND[m] * (np.eye(size, k=m) + np.eye(size, k=-m))
        first += FIRST_SCALE * FIRST[m - 1] * (np.eye(size, k=m) - np.eye(size, k=-m))
    return second, first


def depth_matrix(depth):
    second, first = bands(depth)
    both = np.concatenate([second.T, first.T], axis=1)
    return jnp.asarray(np.concatenate([both, both], axis=0), jnp.bfloat16)


def lateral_matrix(size):
    rows = [np.kron(np.eye(REACH), band) for band in bands(size)]
    return jnp.asarray(np.concatenate([np.concatenate([r, r], axis=1) for r in rows], axis=0), jnp.bfloat16)


def sine_cosine(angle):
    half = 0.5 * angle
    square = half * half

    def series(first, count):
        value = jnp.full_like(square, (-1) ** (count - 1) / math.factorial(2 * count - 2 + first))
        for k in range(count - 2, -1, -1):
            value = value * square + (-1) ** k / math.factorial(2 * k + first)
        return value

    sine = half * series(1, 7)
    return 2.0 * sine * series(0, 8), 1.0 - 2.0 * sine * sine


def swapped(block, axis, bit):
    count = lax.axis_size(axis)
    return lax.ppermute(block, axis, [(i, i ^ bit) for i in range(count)])


def window(place, tile, halo, total, unit):
    count = total // tile
    length = 0
    for i in range(count):
        low = max(0, i * tile - halo) // unit * unit
        high = -(-min(total, (i + 1) * tile + halo) // unit) * unit
        length = max(length, high - low)
    start = jnp.clip((place * tile - halo) // unit * unit, 0, total - length)
    return start, length


def pair_sums(load, tail):
    total = load(1) + load(-1)
    for m, c in enumerate(tail, 2):
        total = total + c * (load(m) + load(-m))
    return total


def pair_differences(load, tail):
    total = load(1) - load(-1)
    for m, b in enumerate(tail, 2):
        total = total + b * (load(m) - load(-m))
    return total


def pack_kernel(*refs):
    waves, earth, out_ref, sems = refs[:4], refs[4:9], refs[9], refs[10]
    tile_x = waves[0].shape[1]
    half = tile_x // 2
    first = lax.axis_index("sec") * half
    copies = []
    for number, ref in enumerate(waves):
        copies.append((ref.at[0], out_ref.at[pl.ds(number * tile_x, tile_x)]))
    for number, ref in enumerate(earth):
        copies.append((ref.at[pl.ds(first, half)], out_ref.at[pl.ds(4 * tile_x + number * half, half)]))
    copies = [pltpu.make_async_copy(a, b, sems.at[i]) for i, (a, b) in enumerate(copies)]
    for copy in copies:
        copy.start()
    for copy in copies:
        copy.wait()


def split(values):
    high = values.astype(jnp.bfloat16)
    return high, (values - high.astype(jnp.float32)).astype(jnp.bfloat16)


def steps_kernel(sizes, plan_ref, depth_ref, lateral_ref, *refs):
    tile_x, tile_y, total_x, total_y, depth, slots, nsnap = sizes
    tiles = refs[: len(slots)]
    halves = [ref.at[i] for ref in refs[len(slots) : len(slots) + 2] for i in range(ref.shape[0])]
    p_out, q_out, snap_out = refs[len(slots) + 2 : len(slots) + 5]
    pa, pb, qa, qb, slope_a, slope_b, rest_a, rest_b, weights, kept = refs[len(slots) + 5 :]
    gx, gy, sec = lax.axis_index("gx"), lax.axis_index("gy"), lax.axis_index("sec")
    half = tile_x // 2
    blocks = total_x // REACH
    size = REACH * total_y

    slopes = [ref.at[i, f] for ref in (slope_a, slope_b) for i in (0, 1) for f in (0, 1)]
    for ref in (pa, pb, qa, qb, *slopes):
        for start in (0, total_x + REACH):
            ref[start : start + REACH] = jnp.zeros((REACH, total_y, depth), jnp.float32)

    for slot, (kx, ky) in enumerate(slots):
        ix, iy = jnp.bitwise_xor(gx, kx), jnp.bitwise_xor(gy, ky)
        xs = ix * tile_x
        ys = pl.ds(pl.multiple_of(iy * tile_y, ROWS), tile_y)
        for number, ref in enumerate((pa, pb, qa, qb)):
            ref[pl.ds(xs + REACH, tile_x), ys] = tiles[slot][number * tile_x : (number + 1) * tile_x]
        for side in (0, 1):
            source = halves[slot] if side else tiles[slot].at[4 * tile_x :]
            base = xs + half * (jnp.bitwise_xor(sec, side))
            for row in range(half):
                courant, epsilon, delta, tilt, azimuth = (source[g * half + row] for g in range(5))
                sin_t, cos_t = sine_cosine(tilt)
                sin_a, cos_a = sine_cosine(azimuth)
                axis_x, axis_y = sin_t * cos_a, sin_t * sin_a
                near, curve = courant * SECOND[1], courant * (1.0 / SECOND_SCALE)
                cross = courant * (2.0 * FIRST[0] / FIRST_SCALE)
                xx, yy, zz = axis_x * axis_x, axis_y * axis_y, cos_t * cos_t
                fields = (
                    near * xx,
                    curve * yy,
                    curve * zz,
                    near - near * xx,
                    curve - curve * yy,
                    curve - curve * zz,
                    cross * axis_x * axis_y,
                    courant * (2.0 / (FIRST_SCALE * FIRST_SCALE)) * axis_y * cos_t,
                    cross * axis_x * cos_t,
                    courant * SECOND[0],
                    1.0 + 2.0 * epsilon,
                    1.0 + 2.0 * delta,
                )
                for number, field in enumerate(fields):
                    weights[number, base + row, ys] = field

    def lateral(first, last, parts):
        matrix = lateral_ref[first * size : last * size]
        return jnp.dot(matrix, jnp.concatenate(parts, axis=0), preferred_element_type=jnp.float32)

    def put(ref, number, rows, values):
        for f in (0, 1):
            ref[number, f, rows] = values[:, f * depth : (f + 1) * depth].reshape(REACH, total_y, depth)

    def prepare(block, fields, slope, rest):
        x = block * REACH
        inner, outer = pl.ds(x, REACH), pl.ds(x + REACH, REACH)
        high, low = split(jnp.concatenate([ref[outer].reshape(size, depth) for ref in fields], axis=0))
        beside = lambda v: jnp.concatenate([v[:size], v[size:]], axis=1)
        out = jnp.dot(
            jnp.concatenate([high, low], axis=1), depth_ref[...], preferred_element_type=jnp.float32
        )
        along_y = lateral(0, 2, [beside(high), beside(low)])
        along_z = beside(out[:, depth:])
        put(rest, 0, inner, along_y[:size])
        put(rest, 1, inner, beside(out[:, :depth]))
        put(slope, 0, outer, along_y[size:])
        put(slope, 1, outer, along_z)
        put(rest, 2, inner, lateral(1, 2, split(along_z)))

    def update(block, now, before, slope, rest, y_low, y_length):
        for lane in range(REACH):
            x = block * REACH + lane
            row = x + REACH
            for j in range(0, y_length, ROWS):
                ys = pl.ds(y_low + j, ROWS)
                w = [weights[i, x, ys] for i in range(12)]
                curves, shears = [], []
                for f in (0, 1):
                    curve_xx = pair_sums(lambda m: now[f][row + m, ys], SECOND_TAIL)
                    curve_xy = pair_differences(lambda m: slope[0, f, row + m, ys], FIRST_TAIL)
                    curve_xz = pair_differences(lambda m: slope[1, f, row + m, ys], FIRST_TAIL)
                    curve_yy, curve_zz, curve_yz = (rest[i, f, x, ys] for i in range(3))
                    u = w[3:6] if f == 0 else w[0:3]
                    curves.append(u[0] * curve_xx + u[1] * curve_yy + u[2] * curve_zz)
                    shears.append(w[6] * curve_xy + w[7] * curve_yz + w[8] * curve_xz)
                p, q = now[0][row, ys], now[1][row, ys]
                p = p + p
                flat = curves[0] - shears[0] + w[9] * p
                axial = curves[1] + shears[1] + w[9] * q
                before[0][row, ys] = p - before[0][row, ys] + w[10] * flat + axial
                before[1][row, ys] = (q + q) - before[1][row, ys] + w[11] * flat + axial

    mine = pl.ds(pl.multiple_of(gy * tile_y, ROWS), tile_y)

    def keep(step, field):
        slot = nsnap
        for j in range(nsnap):
            slot = jnp.where(plan_ref[j] == step, j, slot)
        kept[slot] = field[pl.ds(gx * tile_x, tile_x + 2 * REACH), mine]

    even = ((pa, qa), slope_a, rest_a)
    odd = ((pb, qb), slope_b, rest_b)
    for block in range(blocks - 1):
        prepare(block, *even)

    now, ahead, last = even, odd, blocks - 1
    for step in range(1, STEPS + 1):
        left = REACH * (STEPS - step)
        x_low, x_length = window(gx, tile_x, left + REACH, total_x, REACH)
        y_low, y_length = window(gy, tile_y, left, total_y, ROWS)
        first = 0 if x_length == total_x else x_low // REACH
        y_low = 0 if y_length == total_y else pl.multiple_of(y_low, ROWS)
        count = x_length // REACH
        if count < 3:
            prepare(last, *now)
        for number in range(count):
            update(first + number, now[0], ahead[0], now[1], now[2], y_low, y_length)
            if number == 0 and count >= 3:
                prepare(last, *now)
            if number and step < STEPS:
                prepare(first + number - 1, *ahead)
        last = first + count - 1
        now, ahead = ahead, now
        keep(step, now[0][0])

    snap_out[...] = kept[:nsnap]
    p_out[0] = now[0][0][pl.ds(gx * tile_x + REACH, tile_x), mine]
    q_out[0] = now[0][1][pl.ds(gx * tile_x + REACH, tile_x), mine]


def image_kernel(numbers_ref, own_ref, other_ref, p_ref, q_ref, p_out, q_out, image_ref, sems):
    copies = [
        pltpu.make_async_copy(a, b, sems.at[i]) for i, (a, b) in enumerate(((p_ref, p_out), (q_ref, q_out)))
    ]
    for copy in copies:
        copy.start()
    sec = lax.axis_index("sec")
    sign = 1 - 2 * sec
    nlag, tile_x, tile_y, half = image_ref.shape
    nsnap = own_ref.shape[0]
    for k in range(nlag):
        shift = sign * numbers_ref[nsnap + k]
        total = own_ref[0, pl.ds(REACH - shift, tile_x)] * other_ref[0, pl.ds(REACH + shift, tile_x)]
        for j in range(1, nsnap):
            total = total + own_ref[j, pl.ds(REACH - shift, tile_x)] * other_ref[j, pl.ds(REACH + shift, tile_x)]
        flat = total.reshape(tile_x * tile_y, 2 * half)
        chosen = jnp.where(sec == 0, flat, pltpu.roll(flat, half, 1))
        image_ref[k] = chosen[:, :half].reshape(tile_x, tile_y, half)
    for copy in copies:
        copy.wait()


def gathered_solution(pressure, pressure_before, quasi, quasi_before, courant, epsilon, delta, tilt, azimuth, plan, lags):
    count_x, count_y = lax.axis_size("gx"), lax.axis_size("gy")
    _, tile_x, tile_y, depth = pressure.shape
    total_x, total_y = count_x * tile_x, count_y * tile_y
    half = tile_x // 2
    vmem = pl.BlockSpec(memory_space=pltpu.VMEM)
    smem = pl.BlockSpec(memory_space=pltpu.SMEM)
    apart = pl.BlockSpec(memory_space=pl.ANY)

    parts = (pressure, pressure_before, quasi, quasi_before, courant, epsilon, delta, tilt, azimuth)
    packed = pl.pallas_call(
        pack_kernel,
        out_shape=jax.ShapeDtypeStruct((4 * tile_x + 5 * half, tile_y, depth), jnp.float32),
        in_specs=[apart] * len(parts),
        out_specs=vmem,
        scratch_shapes=[pltpu.SemaphoreType.DMA((len(parts),))],
    )(*parts)
    held = {(0, 0): packed}
    for ky in range(count_y):
        if ky:
            low = ky & -ky
            held[0, ky] = swapped(held[0, ky ^ low], "gy", low)
    for kx in range(1, count_x):
        low = kx & -kx
        rest = kx ^ low
        held[kx, 0] = swapped(held[rest, 0] if rest else held[0, 0], "gx", low)
    for ky in range(1, count_y):
        for kx in range(1, count_x):
            low = ky & -ky
            if kx == 1:
                held[kx, ky] = swapped(held[0, ky], "gx", 1)
            else:
                held[kx, ky] = swapped(held[kx, ky ^ low], "gy", low)
    slots = tuple(held)
    tiles = list(held.values())
    direct = [s for s in slots if 0 in s and all(k & (k - 1) == 0 for k in s)]
    relayed = [s for s in slots if s not in direct]
    slots = tuple(direct + relayed)
    tiles = [held[s] for s in slots]
    others = [swapped(jnp.stack([held[s][4 * tile_x :] for s in part]), "sec", 1) for part in (direct, relayed)]

    numbers = jnp.concatenate([plan, lags])
    nsnap = plan.shape[0]
    sizes = (tile_x, tile_y, total_x, total_y, depth, slots, nsnap)
    field = pltpu.VMEM((total_x + 2 * REACH, total_y, depth), jnp.float32)
    slope = pltpu.VMEM((2, 2, total_x + 2 * REACH, total_y, depth), jnp.float32)
    rest = pltpu.VMEM((3, 2, total_x, total_y, depth), jnp.float32)
    p_last, q_last, snaps = pl.pallas_call(
        functools.partial(steps_kernel, sizes),
        out_shape=(
            jax.ShapeDtypeStruct(pressure.shape, jnp.float32),
            jax.ShapeDtypeStruct(quasi.shape, jnp.float32),
            jax.ShapeDtypeStruct((nsnap, tile_x + 2 * REACH, tile_y, depth), jnp.float32),
        ),
        in_specs=[smem, vmem, vmem] + [vmem] * (len(tiles) + 2),
        out_specs=(vmem, vmem, vmem),
        scratch_shapes=[
            field, field, field, field,
            slope, slope, rest, rest,
            pltpu.VMEM((12, total_x, total_y, depth), jnp.float32),
            pltpu.VMEM((nsnap + 1, tile_x + 2 * REACH, tile_y, depth), jnp.float32),
        ],
        compiler_params=pltpu.CompilerParams(vmem_limit_bytes=24 * 1024 * 1024),
    )(numbers, depth_matrix(depth), lateral_matrix(total_y), *tiles, *others)

    other_snaps = swapped(snaps, "sec", 1)
    p_final, q_final, image = pl.pallas_call(
        image_kernel,
        out_shape=(
            jax.ShapeDtypeStruct(pressure.shape, jnp.float32),
            jax.ShapeDtypeStruct(quasi.shape, jnp.float32),
            jax.ShapeDtypeStruct((lags.shape[0], tile_x, tile_y, depth // 2), jnp.float32),
        ),
        in_specs=[smem] + [vmem] * 4,
        out_specs=(apart, apart, vmem),
        scratch_shapes=[pltpu.SemaphoreType.DMA((2,))],
        compiler_params=pltpu.CompilerParams(vmem_limit_bytes=8 * 1024 * 1024),
    )(numbers, snaps, other_snaps, p_last, q_last)
    return (p_final, q_final, image)


def with_halo(cells, sides, width):
    for axis, dim in sides:
        count = lax.axis_size(axis)
        ends = count - 1
        head = lax.slice_in_dim(cells, 0, width, axis=dim)
        tail = lax.slice_in_dim(cells, cells.shape[dim] - width, cells.shape[dim], axis=dim)
        cells = jnp.concatenate(
            [
                lax.ppermute(tail, axis, [(i, (i + 1) % count) for i in range(ends)]),
                cells,
                lax.ppermute(head, axis, [((i + 1) % count, i) for i in range(ends)]),
            ],
            axis=dim,
        )
    return cells


def from_behind(block, axis, distance):
    devices = range(lax.axis_size(axis))
    route = [(i - distance, i) for i in devices if i - distance in devices]
    return lax.ppermute(block, axis, route)


def second_along(values, dimension):
    amount = values.shape[dimension] - 8
    result = SECOND[0] * lax.slice_in_dim(values, 4, 4 + amount, axis=dimension)
    for offset in range(1, 5):
        result = result + SECOND[offset] * (
            lax.slice_in_dim(values, 4 + offset, 4 + offset + amount, axis=dimension)
            + lax.slice_in_dim(values, 4 - offset, 4 - offset + amount, axis=dimension)
        )
    return result


def first_along(values, dimension):
    amount = values.shape[dimension] - 8
    result = FIRST[0] * (
        lax.slice_in_dim(values, 5, 5 + amount, axis=dimension)
        - lax.slice_in_dim(values, 3, 3 + amount, axis=dimension)
    )
    for offset in range(2, 5):
        result = result + FIRST[offset - 1] * (
            lax.slice_in_dim(values, 4 + offset, 4 + offset + amount, axis=dimension)
            - lax.slice_in_dim(values, 4 - offset, 4 - offset + amount, axis=dimension)
        )
    return result


def trimmed(values, dimensions):
    for dimension in dimensions:
        values = lax.slice_in_dim(values, 4, values.shape[dimension] - 4, axis=dimension)
    return values


def orientation(tilt, azimuth):
    sin_tilt = jnp.sin(tilt)
    cos_tilt = jnp.cos(tilt)
    sin_azim = jnp.sin(azimuth)
    cos_azim = jnp.cos(azimuth)
    square_sin = sin_tilt * sin_tilt
    double_tilt = jnp.sin(2.0 * tilt)
    return (
        square_sin * cos_azim * cos_azim,
        square_sin * sin_azim * sin_azim,
        cos_tilt * cos_tilt,
        square_sin * jnp.sin(2.0 * azimuth),
        double_tilt * sin_azim,
        double_tilt * cos_azim,
    )


def tilted_terms(padded, weights):
    curve_xx = trimmed(second_along(padded, 1), (2, 3))
    curve_yy = trimmed(second_along(padded, 2), (1, 3))
    curve_zz = trimmed(second_along(padded, 3), (1, 2))
    slope_x = first_along(padded, 1)
    slope_y = first_along(padded, 2)
    curve_xy = trimmed(first_along(slope_x, 2), (3,))
    curve_xz = trimmed(first_along(slope_x, 3), (2,))
    curve_yz = trimmed(first_along(slope_y, 3), (1,))
    axial = (
        weights[0] * curve_xx
        + weights[1] * curve_yy
        + weights[2] * curve_zz
        + weights[3] * curve_xy
        + weights[4] * curve_yz
        + weights[5] * curve_xz
    )
    laplace = curve_xx + curve_yy + curve_zz
    return (axial, laplace)


def advance(now_p, before_p, now_q, before_q, axial_p, laplace_p, axial_q, courant, epsilon, delta):
    flat_p = laplace_p - axial_p
    next_p = 2.0 * now_p - before_p + courant * ((1.0 + 2.0 * epsilon) * flat_p + axial_q)
    next_q = 2.0 * now_q - before_q + courant * ((1.0 + 2.0 * delta) * flat_p + axial_q)
    return (next_p, next_q)


def offset_image(paired, lags):
    rim_width = paired.shape[2]
    padded = with_halo(paired, (("gx", 2),), rim_width)
    images = []
    for offset_index in range(lags.shape[0]):
        lag_cells = lags[offset_index]
        source = lax.dynamic_slice_in_dim(padded[0], rim_width - lag_cells, rim_width, 1)
        receiver = lax.dynamic_slice_in_dim(padded[1], rim_width + lag_cells, rim_width, 1)
        images.append(jnp.sum(source * receiver, axis=0))
    return jnp.stack(images)


def stepwise_solution(pressure, pressure_before, quasi, quasi_before, courant, epsilon, delta, tilt, azimuth, plan, lags):
    weights = orientation(tilt, azimuth)
    snapshots = jnp.zeros((plan.shape[0],) + pressure.shape[1:], jnp.float32)
    for step in range(STEPS):
        stacked = jnp.concatenate([pressure, quasi], 0)
        padded = with_halo(stacked, (("gx", 1), ("gy", 2)), 4)
        padded = jnp.pad(padded, ((0, 0), (0, 0), (0, 0), (4, 4)))
        axial, laplace = tilted_terms(padded, weights)
        next_p, next_q = advance(
            pressure, pressure_before, quasi, quasi_before,
            axial[0:1], laplace[0:1], axial[1:2], courant, epsilon, delta,
        )
        pressure_before, quasi_before = (pressure, quasi)
        pressure, quasi = (next_p, next_q)
        picked = (plan == step + 1).astype(jnp.float32)
        snapshots = snapshots + picked[:, None, None, None] * pressure
    arrived = from_behind(snapshots, "sec", 1)
    paired = jnp.stack([arrived, snapshots])
    whole_image = offset_image(paired, lags)
    half_depth = whole_image.shape[3] // 2
    returned = from_behind(whole_image[..., :half_depth], "sec", -1)
    image = jnp.where(lax.axis_index("sec") == 0, returned, whole_image[..., half_depth:])
    return (pressure, quasi, image)


def on_device(*args):
    count_x, count_y = lax.axis_size("gx"), lax.axis_size("gy")
    _, tile_x, tile_y, depth = args[0].shape
    cells = count_x * tile_x * count_y * tile_y * depth
    fits = (
        cells <= 1 << 16
        and count_x * tile_x <= 8 * REACH
        and count_x & (count_x - 1) == 0
        and count_y & (count_y - 1) == 0
        and tile_x % REACH == 0
        and tile_y % ROWS == 0
        and depth == 128
    )
    return (gathered_solution if fits else stepwise_solution)(*args)


def solution(mesh):
    wave = P("sec", ("group", "gx"), "gy", None)
    earth = P("gx", "gy", None)
    return jax.shard_map(
        on_device,
        mesh=mesh,
        in_specs=(wave,) * 4 + (earth,) * 5 + (P(), P()),
        out_specs=(wave, wave, P(None, ("group", "gx"), "gy", "sec")),
        check_vma=False,
    )
```
